128 devices in a mesh: dp: 8 (over x, core), blk: 16 (over y, z).
Axes of the slice: x: 4, y: 4, z: 4, core: 2. Of those that a mesh axis runs over, the one named last changes fastest.
Arguments:
- tokens: bfloat16 [8, 2048, 768], P('dp', 'blk'), may hold values from -6 to 6
- lengths: int32 [8], P('dp'), may hold values from 1024 to 2048, as said below
- w_qkv: bfloat16 [768, 2304], P(('dp', 'blk')), may hold values from -0.3125 to 0.3125
- w_out: bfloat16 [768, 768], P(('dp', 'blk')), may hold values from -0.875 to 0.875
- norm_gain: bfloat16 [768], P(('dp', 'blk')), may hold values from 0.5 to 1.5
- norm_shift: bfloat16 [768], P(('dp', 'blk')), may hold values from -3 to 3
- w_up: bfloat16 [768, 3072], P(('dp', 'blk')), may hold values from -0.21875 to 0.21875
- w_down: bfloat16 [3072, 768], P(('dp', 'blk')), may hold values from -0.109375 to 0.109375
- cotangent: bfloat16 [8, 2048, 768], P('dp', 'blk'), may hold values from -6 to 6
Outputs:
- output: bfloat16 [8, 2048, 768], P('dp', 'blk')
- d_tokens: float32 [8, 2048, 768], P('dp', 'blk')
- d_qkv: float32 [768, 2304], P(('dp', 'blk'))
- d_out: float32 [768, 768], P(('dp', 'blk'))
- d_gain: float32 [768], P(('dp', 'blk'))
- d_shift: float32 [768], P(('dp', 'blk'))
- d_up: float32 [768, 3072], P(('dp', 'blk'))
- d_down: float32 [3072, 768], P(('dp', 'blk'))
The draws below stay inside these ranges and needn't reach their ends.
Inputs may be any that keep to these rules, and one draw needn't show every extreme that they name: `lengths`: each group's value is 2048 (one sequence filling the group) or 2048 // 2 (two sequences of that length, one after the other); both kinds occur in every draw.
All inputs are finite; a program needn't handle non-finite values.
Results may differ from the reference program's by a relative error of at most 0.024.
Values may be sent and summed in bfloat16 or wider, within the bound.
A program may use at most 128 MiB of HBM per device.

```python
import math
import jax
import jax.numpy as jnp
from jax import lax

D = 768
H = 12
HD = 64
FF = 3072
GROUP_LEN = 2048
GROUPS = 8


def draw_lengths(key, part):
    key = jax.random.fold_in(key, 11)
    kind_key, long_key, short_key = jax.random.split(key, 3)
    kinds = jax.random.randint(kind_key, (GROUPS,), 0, 2)
    long_at = jax.random.randint(long_key, (), 0, GROUPS)
    short_at = (long_at + jax.random.randint(short_key, (), 1, GROUPS)) % GROUPS
    slots = jnp.arange(GROUPS)
    kinds = jnp.where(slots == long_at, 1, jnp.where(slots == short_at, 0, kinds))
    return jnp.where(kinds == 1, GROUP_LEN, GROUP_LEN // 2).astype(jnp.int32)


def level_of(key, dims, cuts, least, top_value):
    def one(axis_at, parts):
        steps = jax.random.uniform(jax.random.fold_in(jax.random.fold_in(key, 6), axis_at), (parts,), jnp.float32, least / len(cuts), top_value / len(cuts))
        return jnp.repeat(jnp.exp(steps), dims[axis_at] // parts).reshape((-1,) + (1,) * (len(dims) - axis_at - 1))

    gain = one(*cuts[0])
    for cut in cuts[1:]:
        gain = gain * one(*cut)
    return gain


def scatter_about(own_key, dims, scale, bound, cuts=(), held_as=jnp.bfloat16):
    factor_of = level_of(own_key, dims, cuts, -0.22, 0.18) if cuts else 1.0
    array = jax.random.normal(own_key, dims, jnp.float32) * scale * factor_of
    return jnp.minimum(jnp.maximum(array, -bound), bound).astype(held_as)


def setup_inputs(seed: int = 0) -> dict:
    key_of = jax.random.split(jax.random.key(seed), 10)
    return {
        "tokens": scatter_about(key_of[0], (GROUPS, GROUP_LEN, D), 1.0, 6.0, ((0, 8), (1, 16))),
        "lengths": draw_lengths(jax.random.fold_in(key_of[9], 71), 0),
        "w_qkv": scatter_about(key_of[2], (D, 3 * D), (D // 2) ** -0.5, 0.3125, ((0, 128),)),
        "w_out": scatter_about(key_of[3], (D, D), (D // 16) ** -0.5, 0.875, ((0, 128),)),
        "norm_gain": jnp.clip(1.0 + 0.1 * jax.random.normal(key_of[4], (D,), jnp.float32), 0.5, 1.5).astype(jnp.bfloat16),
        "norm_shift": scatter_about(key_of[5], (D,), 0.5, 3.0, ((0, 128),)),
        "w_up": scatter_about(key_of[6], (D, FF), D ** -0.5, 0.21875, ((0, 128),)),
        "w_down": scatter_about(key_of[7], (FF, D), FF ** -0.5, 0.109375, ((0, 128),)),
        "cotangent": scatter_about(key_of[8], (GROUPS, GROUP_LEN, D), 1.0, 6.0, ((0, 8), (1, 16))),
    }


@jax.custom_vjp
def low(v):
    return lax.optimization_barrier(v.astype(jnp.bfloat16)).astype(jnp.float32)

@jax.custom_vjp
def low_back(v):
    return v

def low_keep(v):
    return (low(v), None)

def low_pass(kept, grad):
    return (grad,)

def back_keep(v):
    return (v, None)

def back_low(kept, grad):
    return (low(grad),)
low.defvjp(low_keep, low_pass)
low_back.defvjp(back_keep, back_low)
highest = lax.Precision.HIGHEST
big_negative = -1e+30

def matmul_hi(left, right):
    return jnp.dot(left, right, precision=highest, preferred_element_type=jnp.float32)

def gelu_tanh(values):
    return jax.nn.gelu(values, approximate=True)

def layer_norm(hidden, gain_vals, shift_vals):
    centred = hidden - lax.optimization_barrier(jnp.mean(hidden, -1, keepdims=True))
    spread = lax.optimization_barrier(jnp.mean(centred * centred, -1, keepdims=True))
    return centred * lax.rsqrt(spread + 1e-05) * gain_vals + shift_vals

def attend_rows(query_block, query_pos, key_rows, value_rows, doc_len):
    scores = jnp.einsum('thd,shd->hts', query_block, key_rows, precision=highest, preferred_element_type=jnp.float32)
    scores = low_back(scores * HD ** (-0.5))
    key_pos = jnp.arange(key_rows.shape[0], dtype=jnp.int32)
    allowed = (key_pos[None, :] <= query_pos[:, None]) & ((key_pos // doc_len)[None, :] == (query_pos // doc_len)[:, None])
    allowed = allowed[None]
    magnitude = jnp.where(allowed, jnp.abs(scores), big_negative)
    row_top = lax.optimization_barrier(jnp.max(magnitude, -1, keepdims=True))
    expo_vals = jnp.where(allowed, jnp.exp(magnitude - row_top), 0.0)
    row_total = lax.optimization_barrier(jnp.sum(expo_vals, -1, keepdims=True))
    weights = low(jnp.sign(scores) * expo_vals / row_total)
    return jnp.einsum('hts,shd->thd', weights, value_rows, precision=highest, preferred_element_type=jnp.float32)

def group_layer(params, inputs, doc_len):
    w_qkv, w_out, gain_vals, shift_vals, w_up, w_down = params
    qkv = low_back(low(matmul_hi(inputs, w_qkv)))
    seq_rows = inputs.shape[0]
    queries = qkv[:, :D].reshape(seq_rows, H, HD)
    key_rows = qkv[:, D:2 * D].reshape(seq_rows, H, HD)
    value_rows = qkv[:, 2 * D:].reshape(seq_rows, H, HD)
    block_rows = math.gcd(seq_rows, 512)
    block_count = seq_rows // block_rows
    positions = jnp.arange(seq_rows, dtype=jnp.int32).reshape(block_count, block_rows)

    def one_block(block_pair):
        return attend_rows(block_pair[0], block_pair[1], key_rows, value_rows, doc_len)
    mixed = lax.map(jax.checkpoint(one_block), (queries.reshape(block_count, block_rows, H, HD), positions))
    attn_vals = low_back(low(mixed.reshape(seq_rows, D)))
    hidden = inputs + low_back(matmul_hi(attn_vals, w_out))
    normed = low(layer_norm(hidden, gain_vals, shift_vals))
    pre_act = low_back(matmul_hi(normed, w_up))
    active = low(gelu_tanh(pre_act))
    return hidden + matmul_hi(active, w_down)

def reference(tokens, lengths, w_qkv, w_out, norm_gain, norm_shift, w_up, w_down, cotangent):
    doc_lens = lengths.astype(jnp.int32)

    def forward(inputs, qkv_w, out_w, gain_w, shift_w, up_w, down_w):
        params = (qkv_w, out_w, gain_w, shift_w, up_w, down_w)

        def one_group(group_pair):
            return group_layer(params, group_pair[0], group_pair[1])
        return lax.map(jax.checkpoint(one_group), (inputs, doc_lens))
    output, pull = jax.vjp(forward, tokens.astype(jnp.float32), w_qkv.astype(jnp.float32), w_out.astype(jnp.float32), norm_gain.astype(jnp.float32), norm_shift.astype(jnp.float32), w_up.astype(jnp.float32), w_down.astype(jnp.float32))
    grads = pull(cotangent.astype(jnp.float32))
    return (output.astype(jnp.bfloat16), grads[0], grads[1], grads[2], grads[3], grads[4], grads[5], grads[6])
```

```python
import jax
import jax.numpy as jnp
from jax import lax
from jax.experimental import pallas as pl
from jax.experimental.pallas import tpu as pltpu
from jax.sharding import PartitionSpec as P

MESH = pl.DeviceIdType.MESH
F32 = jnp.float32
BF16 = jnp.bfloat16
NEG = -1e30
LOG2E = 1.4426950408889634
SCALE = 0.125
EXP_SCALE = SCALE * LOG2E
ORDERS = (((("x", "y", "z"), ("y", "z", "x"), ("z", "x", "y")),) * 3)
TILE = 256
TILES = 8
CHUNKS = 4
HEADS_HERE = 12


def dot(a, b):
    return lax.dot_general(a, b, (((1,), (0,)), ((), ())), preferred_element_type=F32)


def dot_nt(a, b):
    return lax.dot_general(a, b, (((1,), (1,)), ((), ())), preferred_element_type=F32)


def turned(a):
    return a.astype(F32).T.astype(BF16)


def kernel(
    x_hbm, len_ref, wqkv_hbm, wout_hbm, gain_ref, shift_ref, wup_hbm, wdown_hbm, dy_hbm,
    out_hbm, dtok_hbm, dgs_ref, fin_r, ddown_ref,
    wqkv_ref, wout_ref, wup_ref, wdown_ref, out_ref, dtok_ref, g_ref, r_ref, s1p2, s2p2, dp1, dp0, dpl, p_ref,
    xf, dyf, lenf, ps, pr, uq, pds, pdr, ud, gss, gsr, wos,
    qkvt, aq, kn, vn, otf, lse_ref, top_ref, total_ref, delta_ref, acc_ref, otb, oth, of, nf, act, slope, turn_ref, xt_ref, dpre, pdown, dxr, dnp, dnx, dhf,
    dot_s, ado, dkt, dvt, dqs, dqh, dqf, dtp, dtx, hid_ref, fin_s, fds, fdr,
    ag_s, ag_r, lg_s, lg_r, rs_s, rs_r, rl_s, rl_r, pl_s, pl_r, pr_s, pr_r, ps_s, ps_r, ex_s, ex_r, gs_s, gs_r, aq_s, aq_r, ot_s, ot_r, do_s, do_r, dq_s, dq_r,
    fin_ss, fin_rs, in_s,
):
    dp, blk = lax.axis_index("dp"), lax.axis_index("blk")
    x, c = dp // 2, lax.rem(dp, 2)
    y, z = blk // 4, lax.rem(blk, 4)
    other = 1 - c
    coord = {"x": x, "y": y, "z": z}

    def place(cx, cc, cy, cz):
        return (2 * cx + cc, 4 * cy + cz)

    def yp(cy):
        return lax.rem(cy, 2) * 2 + cy // 2

    loads = [
        pltpu.make_async_copy(src, dst, in_s.at[n])
        for n, (src, dst) in enumerate(
            (
                (wqkv_hbm, wqkv_ref), (wout_hbm, wout_ref), (wup_hbm, wup_ref), (wdown_hbm, wdown_ref),
                (x_hbm, xf.at[c]), (dy_hbm, dyf.at[c]),
            )
        )
    ]
    for load in loads:
        load.start()
    sibling = place(x, other, y, z)
    drain = []

    def remote(src, dst, ssem, rsem, dev):
        return pltpu.make_async_remote_copy(
            src_ref=src, dst_ref=dst, send_sem=ssem, recv_sem=rsem, device_id=dev, device_id_type=MESH
        )

    def send(src, dst, ssem, rsem, dev):
        copy = remote(src, dst, ssem, rsem, dev)
        if drain:
            copy.wait_send()
        else:
            copy.start()

    def landed(dst, rsem):
        if not drain:
            remote(dst, dst, rsem, rsem, sibling).wait_recv()

    def send_or_copy(src, dst, ssem, rsem, dev, mine):
        if not drain:

            @pl.when(mine)
            def _():
                pltpu.make_async_copy(src, dst, rsem).start()

        @pl.when(jnp.logical_not(mine))
        def _():
            send(src, dst, ssem, rsem, dev)

    barrier = pltpu.get_barrier_semaphore()
    for cc in range(2):

        @pl.loop(0, 16)
        def _(b):
            @pl.when(jnp.logical_or(cc != c, b != blk))
            def _():
                pl.semaphore_signal(barrier, inc=1, device_id=(2 * x + cc, b), device_id_type=MESH)

    for d in range(1, 4):
        far_x = lax.rem(x + d, 4)
        for n in range(4):
            spots = [place(far_x, c, lax.rem(y + n, 4), z)]
            if n == 0:
                spots.append(place(far_x, other, y, z))
            else:
                spots.append(place(far_x, c, y, lax.rem(z + n, 4)))
            for spot in spots:
                pl.semaphore_signal(barrier, inc=1, device_id=spot, device_id_type=MESH)

    own_rows = pl.ds(pl.multiple_of(128 * c, 128), 128)
    other_rows = pl.ds(pl.multiple_of(128 * other, 128), 128)

    def exchanges():
        exchange(0, xf.at[c], xf.at[c])
        exchange(1, dyf.at[c], dyf.at[c])
        exchange(2, lenf.at[c], lenf.at[c])
        send_out_half()
        for n in range(3):
            send_grad_normed(n)
        exchange(7, dhf.at[c], dhf.at[c])
        exchange(8, pdown.at[other_rows], dxr)
        exchange(9, dtp.at[other], dtx)

    def send_out_half():
        exchange(3, g_ref.at[0, 0, 3], wos.at[0])
        exchange(10, g_ref.at[0, 1, :, 3], wos.at[1])
        exchange(11, g_ref.at[0, 2, :, :, 3], wos.at[2])

    def exchange(i, src, dst):
        send(src, dst, ex_s.at[i], ex_r.at[i], sibling)

    def exchanged(i, dst):
        landed(dst, ex_r.at[i])

    unit_y = 2 * (y // 2) + c
    slot = lax.rem(y, 2) * 4 + z
    half = lax.rem(z, 2)
    partner = place(x, c, y, z + 1 - 2 * half)

    def send_strips():
        for b in range(2):
            for at in range(8):
                cc, zz = at // 4, at % 4
                mine = (c == cc) & (z == zz) & (y == unit_y)
                dev = place(x, cc, unit_y, zz)
                send_or_copy(
                    ps.at[b, at], pr.at[b, slot], ps_s.at[8 * b + at], ps_r.at[8 * b + slot], dev, mine
                )
        send(pds, pdr, ps_s.at[16], ps_r.at[16], partner)

    def fill_strip(b, at):
        cc, zz = at // 4, at % 4
        if b == 1:
            f0 = 384 * (2 * zz + cc)
            strip = wup_ref[:, f0 : f0 + 384]
        elif zz < 3:
            strip = wqkv_ref[:, 768 * zz + 384 * cc : 768 * zz + 384 * cc + 384]
        else:
            strip = wout_ref[:, 384 * cc : 384 * cc + 384]
        ps[b, at, 0:6, :] = strip.astype(F32)
        ps[b, at, 6:8, :] = jnp.zeros((2, 384), F32)

    def rows_stage(u, stage):
        for n in range(1, 8 if stage else 16):
            d0, d1 = divmod(n, 2 if stage else 4)
            if stage:
                dev = place(lax.rem(x + d0, 4), lax.rem(c + d1, 2), y, z)
            else:
                dev = place(x, c, lax.rem(y + d0, 4), lax.rem(z + d1, 4))
            at = n - 1 + 15 * stage
            send(gss.at[u, stage], gsr.at[u, at], gs_s.at[u, at], gs_r.at[u, at], dev)

    def rows_sum(u, stage):
        total = gss[u, stage]
        for n in range(7 if stage else 15):
            at = n + 15 * stage
            landed(gsr.at[u, at], gs_r.at[u, at])
            total = total + gsr[u, at]
        gss[u, stage + 1] = total

    for load in loads:
        load.wait()
    for b in range(2):
        for at in range(8):
            fill_strip(b, at)
    wd_left = wdown_ref[:, 0:384].astype(F32)
    wd_right = wdown_ref[:, 384:768].astype(F32)
    pds[...] = jnp.where(half == 0, wd_right, wd_left)
    lenf[c] = jnp.full((8, TILE), len_ref[0], jnp.int32).astype(F32)
    lane = lax.broadcasted_iota(jnp.int32, (1, 768), 1)
    first = 6 * (dp * 16 + blk)

    def own_entries(ref):
        entries = ref[...].astype(F32)
        spread = jnp.zeros((1, 768), F32)
        for n in range(6):
            spread = jnp.where(lane == first + n, entries[:, n : n + 1], spread)
        return spread

    def put_rows(u, first_row, second_row):
        for n in range(3):
            lanes = slice(256 * n, 256 * n + 256)
            gss[u, 0, n : n + 1, :] = first_row[:, lanes]
            gss[u, 0, n + 3 : n + 4, :] = second_row[:, lanes]
        gss[u, 0, 6:8, :] = jnp.zeros((2, 256), F32)

    def get_rows(u):
        return [jnp.concatenate([gss[u, 2, n + m : n + m + 1, :] for n in range(3)], axis=1) for m in (0, 3)]

    put_rows(0, own_entries(gain_ref), own_entries(shift_ref))
    ud[pl.ds(pl.multiple_of(24 * half, 8), 24), :] = jnp.where(half == 0, wd_left, wd_right)
    pl.semaphore_wait(barrier, 55)
    send_strips()
    rows_stage(0, 0)
    exchange(0, xf.at[c], xf.at[c])
    exchange(1, dyf.at[c], dyf.at[c])
    exchange(2, lenf.at[c], lenf.at[c])

    def piece(ref, b, k, px, py, pz):
        at = {"x": px, "y": py, "z": pz}
        return ref.at[(b, k) + tuple(at[axis] for axis in reversed(ORDERS[b][k]))]

    def chunk(ref, b, k, p, value, half_of=None):
        index = [b, k]
        for level in (2, 1, 0):
            axis = ORDERS[b][k][level]
            at = value if level == p else coord[axis]
            if level >= p:
                index.append(yp(at) if axis == "y" else at)
            elif half_of is not None and level == 1:
                index.append(pl.ds(2 * half_of, 2))
            else:
                index.append(slice(None))
        return ref.at[tuple(index)]

    def ring(b, k, p):
        axis = ORDERS[b][k][p]
        here = coord[axis]
        right, left, far = (lax.rem(here + d, 4) for d in (1, 3, 2))

        def dev(value):
            at = {**coord, axis: value}
            return place(at["x"], c, at["y"], at["z"])

        return here, right, left, far, dev(right), dev(left)

    def sem_at(b, k, p):
        return ((b * 3 + k) * 3 + p) * 4

    def direct(b, k, p):
        axis = ORDERS[b][k][p]
        here = coord[axis]
        for d in range(1, 4):
            ahead_of = lax.rem(here + d, 4)
            at = {**coord, axis: ahead_of}
            yield d - 1, ahead_of, place(at["x"], c, at["y"], at["z"]), lax.rem(here + 4 - d, 4)

    def gather_small(b, p):
        for k in range(3):
            own = chunk(g_ref, b, k, p, coord[ORDERS[b][k][p]])
            i = sem_at(b, k, p)
            for n, _, dev, _ in direct(b, k, p):
                send(own, own, ag_s.at[i + n], ag_r.at[i + n], dev)

    def gather_small_end(b, p):
        for k in range(3):
            i = sem_at(b, k, p)
            for n, _, _, behind in direct(b, k, p):
                landed(chunk(g_ref, b, k, p, behind), ag_r.at[i + n])

    def plane(k):
        first, second, _ = ORDERS[0][k]
        for n in range(1, 16):
            d0, d1 = divmod(n, 4)
            ahead_of = {**coord, first: lax.rem(coord[first] + d0, 4), second: lax.rem(coord[second] + d1, 4)}
            behind = {
                **coord, first: lax.rem(coord[first] + 4 - d0, 4), second: lax.rem(coord[second] + 4 - d1, 4)
            }
            dev = place(ahead_of["x"], c, ahead_of["y"], ahead_of["z"])
            yield n - 1, ahead_of, dev, behind

    def tile_at(ref, b, k, at):
        return piece(ref, b, k, at["x"], yp(at["y"]), at["z"])

    def gather_plane(b):
        for k in range(3):
            own = tile_at(g_ref, b, k, coord)
            for n, _, dev, _ in plane(k):
                send(own, own, pl_s.at[k, n], pl_r.at[k, n], dev)

    def gather_plane_end(b):
        for k in range(3):
            for n, _, _, behind in plane(k):
                landed(tile_at(g_ref, b, k, behind), pl_r.at[k, n])

    def reduce_plane(b):
        for k in range(3):
            for n, ahead_of, dev, _ in plane(k):
                send(tile_at(r_ref, b, k, ahead_of), dpl.at[k, n], pr_s.at[k, n], pr_r.at[k, n], dev)

    def reduce_plane_end(b):
        for k in range(3):
            total = tile_at(r_ref, b, k, coord)[...].astype(F32)
            for n in range(15):
                landed(dpl.at[k, n], pr_r.at[k, n])
                total = total + dpl[k, n].astype(F32)
            p_ref[b, pl.ds(16 * k, 16), :] = total

    def gather_near(b):
        for k in range(3):
            here, right, left, far, to_right, to_left = ring(b, k, 2)
            i = (b * 3 + k) * 6
            for h in range(2):
                part = chunk(g_ref, b, k, 2, here, h)
                send(part, part, lg_s.at[i + h], lg_r.at[i + h], to_right)
                part = chunk(g_ref, b, k, 2, here, 1 - h)
                send(part, part, lg_s.at[i + 3 - h], lg_r.at[i + 3 - h], to_left)

    def gather_far(b):
        for k in range(3):
            here, right, left, far, to_right, to_left = ring(b, k, 2)
            i = (b * 3 + k) * 6
            part = chunk(g_ref, b, k, 2, left, 0)
            landed(part, lg_r.at[i])
            send(part, part, lg_s.at[i + 4], lg_r.at[i + 4], to_right)
            part = chunk(g_ref, b, k, 2, right, 1)
            landed(part, lg_r.at[i + 3])
            send(part, part, lg_s.at[i + 5], lg_r.at[i + 5], to_left)

    def gather_end(b):
        for k in range(3):
            here, right, left, far, to_right, to_left = ring(b, k, 2)
            i = (b * 3 + k) * 6
            landed(chunk(g_ref, b, k, 2, left, 1), lg_r.at[i + 1])
            landed(chunk(g_ref, b, k, 2, right, 0), lg_r.at[i + 2])
            landed(chunk(g_ref, b, k, 2, far, 0), lg_r.at[i + 4])
            landed(chunk(g_ref, b, k, 2, far, 1), lg_r.at[i + 5])

    def add_to(part, term):
        if not drain:
            part[...] = part[...] + term[...]

    def reduce_far(b):
        for k in range(3):
            here, right, left, far, to_right, to_left = ring(b, k, 2)
            i = (b * 3 + k) * 6
            send(chunk(r_ref, b, k, 2, far, 0), s1p2.at[b, k, 0], rl_s.at[i], rl_r.at[i], to_right)
            send(chunk(r_ref, b, k, 2, far, 1), s1p2.at[b, k, 1], rl_s.at[i + 1], rl_r.at[i + 1], to_left)
        for k in range(3):
            here, right, left, far, to_right, to_left = ring(b, k, 2)
            i = (b * 3 + k) * 6 + 2
            into = s2p2.at[b, k, 0, pl.ds(2, 2)]
            send(chunk(r_ref, b, k, 2, right, 1), into, rl_s.at[i], rl_r.at[i], to_right)
            into = s2p2.at[b, k, 1, pl.ds(0, 2)]
            send(chunk(r_ref, b, k, 2, left, 0), into, rl_s.at[i + 1], rl_r.at[i + 1], to_left)

    def reduce_near(b):
        for k in range(3):
            here, right, left, far, to_right, to_left = ring(b, k, 2)
            i = (b * 3 + k) * 6
            for n, (beside, dev) in enumerate(((right, to_right), (left, to_left))):
                landed(s1p2.at[b, k, n], rl_r.at[i + n])
                part = chunk(r_ref, b, k, 2, beside, n)
                add_to(part, s1p2.at[b, k, n])
                into = s2p2.at[b, k, n, pl.ds(2 * n, 2)]
                send(part, into, rl_s.at[i + 4 + n], rl_r.at[i + 4 + n], dev)

    def reduce_end(b):
        for k in range(3):
            here = coord[ORDERS[b][k][2]]
            i = (b * 3 + k) * 6
            for n in range(2):
                landed(s2p2.at[b, k, n, pl.ds(2 - 2 * n, 2)], rl_r.at[i + 2 + n])
                landed(s2p2.at[b, k, n, pl.ds(2 * n, 2)], rl_r.at[i + 4 + n])
            part = chunk(r_ref, b, k, 2, here)
            total = part[...].astype(F32) + s2p2[b, k, 0].astype(F32) + s2p2[b, k, 1].astype(F32)
            part[...] = total.astype(BF16)

    def reduce_small(b, p):
        into = (dp0, dp1)[p]
        for k in range(3):
            i = sem_at(b, k, p)
            for n, ahead_of, dev, _ in direct(b, k, p):
                send(chunk(r_ref, b, k, p, ahead_of), into.at[b, k, n], rs_s.at[i + n], rs_r.at[i + n], dev)

    def reduce_small_end(b, p):
        into = (dp0, dp1)[p]
        for k in range(3):
            i = sem_at(b, k, p)
            part = chunk(r_ref, b, k, p, coord[ORDERS[b][k][p]])
            total = part[...].astype(F32)
            for n in range(3):
                landed(into.at[b, k, n], rs_r.at[i + n])
                total = total + into[b, k, n].astype(F32)
            if p == 0:
                p_ref[b, pl.ds(16 * k, 16), :] = total
            else:
                part[...] = total.astype(BF16)

    def own_unit(b, rows):
        for k in range(3):
            piece(g_ref, b, k, x, yp(y), z)[...] = rows[16 * k : 16 * k + 16]

    def unit(b):
        for n in range(8):
            landed(pr.at[b, n], ps_r.at[8 * b + n])
            uq[b, 6 * n : 6 * n + 6, :] = pr[b, n, 0:6, :]
        own_unit(b, uq[b].astype(BF16))

    unit(0)
    gather_plane(0)
    landed(pdr, ps_r.at[16])
    ud[pl.ds(pl.multiple_of(24 * (1 - half), 8), 24), :] = pdr[...]
    own_unit(2, ud[...].astype(BF16))
    exchanged(0, xf.at[other])

    unit(1)
    gather_small(1, 0)
    gather_small(2, 0)
    gather_plane_end(0)
    rows_sum(0, 0)
    rows_stage(0, 1)
    gather_near(0)
    x_all = xf[...].reshape(256, 768)
    xt_ref[...] = turned(x_all)
    gather_small_end(1, 0)
    gather_small_end(2, 0)
    gather_far(0)
    gather_small(1, 1)
    gather_small(2, 1)
    gather_end(0)

    units = [(px, py) for px in range(4) for py in range(4)]

    def rows_of(b, j, at):
        return jnp.concatenate([piece(g_ref, b, k, px, py, j)[...] for px, py in at for k in range(3)], axis=0)

    def weight(b, j):
        return rows_of(b, j, units)

    def put(b, j, at, rows):
        for n, (px, py) in enumerate(at):
            for k in range(3):
                start = 48 * n + 16 * k
                piece(r_ref, b, k, px, py, j)[...] = rows[start : start + 16]

    def other_half(at):
        parts = [wos[k, px, py] if k == 1 else wos[k, py, px] for px, py in at for k in range(3)]
        return jnp.concatenate(parts, axis=0)

    x_all = xf[...].reshape(256, 768)

    part = dot(x_all, jnp.concatenate([weight(0, j) for j in range(3)], axis=1)).astype(BF16).astype(F32)
    for j in range(3):
        for g in range(2):
            flat = part[128 * g : 128 * g + 128, 384 * j : 384 * j + 384].T.astype(BF16)
            for h in range(6):
                qkvt[6 * g + h, j] = flat[64 * h : 64 * h + 64]

    turn = 3 * y + 3 + z

    def owner_place(cc, m):
        oy = m // 3
        n = lax.rem(m, 3)
        oz = n + jnp.where(n < 3 - oy, 0, 1)
        return place(x, cc, oy, oz), (y == oy) & (z == oz) & (c == cc)

    def send_heads():
        for n in range(HEADS_HERE):
            m = lax.rem(turn + n, HEADS_HERE)
            dev, mine = owner_place(c, m)
            send_or_copy(qkvt.at[m], aq.at[blk], aq_s.at[m], aq_r.at[blk], dev, mine)

    send_heads()
    send_out_half()
    gather_small_end(1, 1)
    gather_near(1)
    gather_small_end(2, 1)
    gather_near(2)

    owner = z != 3 - y
    group = y // 2
    head_slot = 3 * y + z - jnp.where(z > 3 - y, 1, 0)
    exchanged(2, lenf.at[other])

    def blocks_of(ref, first_block, count, j=None):
        at = [first_block + n for n in range(count)]
        return jnp.concatenate([ref[n] if j is None else ref[n, j] for n in at], axis=1)

    def split_bias(ii, kt):
        short = lenf[group, 0:1, :] < 1536.0
        apart = jnp.logical_and(ii >= CHUNKS // 2, kt < CHUNKS // 2)
        return jnp.where(jnp.logical_and(short, apart), NEG, 0.0)

    def sign_of(scores):
        return jnp.clip(scores * 3e38, -1.0, 1.0)

    key_at = lax.broadcasted_iota(jnp.int32, (TILE, TILE), 0)
    query_at = lax.broadcasted_iota(jnp.int32, (TILE, TILE), 1)

    def heads_home(b):
        hy, hz = b // 4, lax.rem(b, 4)
        for cc in range(2):
            mine = (c == cc) & (y == hy) & (z == hz)
            dev = place(x, cc, hy, hz)
            send_or_copy(otb.at[b], oth.at[c, head_slot], ot_s.at[cc, b], ot_r.at[c, head_slot], dev, mine)

    def grads_home(b):
        hy, hz = b // 4, lax.rem(b, 4)
        mine = (y == hy) & (z == hz)
        send_or_copy(
            dqs.at[b], dqh.at[head_slot], dq_s.at[b], dq_r.at[head_slot], place(x, c, hy, hz), mine
        )

    def allowed(size):
        return jnp.where(key_at <= query_at, size, NEG)

    def forward_step(ii, kt, on_diagonal):
        queries = blocks_of(aq, 4 * ii, 4, 0)
        scores = [dot(kn[2 * kt], queries)]
        if on_diagonal:
            later = dot(kn[2 * kt + 1], queries[:, TILE:])
            scores = [[scores[0][:, 0:TILE]], [scores[0][:, TILE:], later]]
            bias = 0.0
        else:
            scores.append(dot(kn[2 * kt + 1], queries))
            scores = [[s[:, TILE * h : TILE * h + TILE] for s in scores] for h in range(2)]
            bias = split_bias(ii, kt)
        for h in range(2):
            size = [jnp.abs(s) * EXP_SCALE for s in scores[h]]
            if on_diagonal:
                size[h] = allowed(size[h])
            most = jnp.max(size[0], axis=0, keepdims=True)
            for more in size[1:]:
                most = jnp.maximum(most, jnp.max(more, axis=0, keepdims=True))
            if on_diagonal:
                top = most
                total = jnp.zeros((1, TILE), F32)
                acc = jnp.zeros((64, TILE), F32)
            else:
                top = jnp.maximum(top_ref[h], most + bias)
                rescale = jnp.exp2(top_ref[h] - top)
                total = total_ref[h] * rescale
                acc = acc_ref[h] * rescale
            for n in range(len(size)):
                expo = jnp.exp2(size[n] - (top - bias))
                total = total + jnp.sum(expo, axis=0, keepdims=True)
                weights = (expo * sign_of(scores[h][n])).astype(BF16)
                acc = acc + dot(blocks_of(aq, 4 * kt + 2 * n, 2, 2), weights)
            top_ref[h] = top
            total_ref[h] = total
            acc_ref[h] = acc

    def forward_first(ii):
        for b in range(4):
            landed(aq.at[4 * ii + b], aq_r.at[4 * ii + b])
        for n in range(2):
            kn[2 * ii + n] = turned(blocks_of(aq, 4 * ii + 2 * n, 2, 1))
            vn[2 * ii + n] = turned(blocks_of(aq, 4 * ii + 2 * n, 2, 2))
        forward_step(ii, ii, True)

    def forward_last(ii):
        for h in range(2):
            heads = acc_ref[h] / total_ref[h]
            otf[2 * ii + h] = heads
            lse_ref[2 * ii + h] = top_ref[h] + jnp.log(total_ref[h]) * LOG2E
            heads = heads.astype(BF16)
            for b in range(2):
                otb[4 * ii + 2 * h + b] = heads[:, 128 * b : 128 * b + 128]
        for n in range(4):
            heads_home(4 * ii + lax.rem(z + n, 4))

    def run_steps(first, step, last, at_first, at_step):
        @pl.loop(0, CHUNKS)
        def _(n):
            ii = n if first is forward_first else CHUNKS - 1 - n

            @pl.when(owner)
            def _():
                first(ii)

            for at, work in at_first.items():
                pl.when(n == at)(lambda work=work: (work(), None)[1])

            @pl.loop(0, ii)
            def _(t):
                @pl.when(owner)
                def _():
                    step(ii, ii - 1 - t, False)

                for (at, at_t), work in at_step.items():
                    pl.when((n == at) & (t == at_t))(lambda work=work: (work(), None)[1])

            @pl.when(owner)
            def _():
                last(ii)

    run_steps(
        forward_first,
        forward_step,
        forward_last,
        {},
        {},
    )
    gather_far(1)
    gather_far(2)

    def from_heads(ref, g):
        return jnp.concatenate([ref[6 * g + h] for h in range(6)], axis=0).astype(F32).T.astype(BF16)

    for h in range(2):
        for m in range(HEADS_HERE):
            landed(oth.at[h, m], ot_r.at[h, m])
        for g in range(2):
            of[h, 128 * g : 128 * g + 128, :] = from_heads(oth.at[h], g)
    for n, k in ((3, 0), (10, 1), (11, 2)):
        exchanged(n, wos.at[k])
    rows_sum(0, 1)
    gain, shift = get_rows(0)

    def normal(hidden):
        centred = hidden - jnp.mean(hidden, axis=1, keepdims=True)
        inv = lax.rsqrt(jnp.mean(centred * centred, axis=1, keepdims=True) + 1e-05)
        return centred * inv, inv

    attn = jnp.concatenate([of[0], of[1]], axis=1)
    by_both = dot(attn, jnp.concatenate([weight(0, 3), other_half(units)], axis=1))
    by_own, by_other = by_both[:, 0:384], by_both[:, 384:768]
    mixed = jnp.concatenate(
        [jnp.where(c == 0, by_own, by_other), jnp.where(c == 0, by_other, by_own)], axis=1
    )
    hid_ref[...] = x_all.astype(F32) + mixed
    nf[...] = (normal(hid_ref[...])[0] * gain + shift).astype(BF16)
    exchanged(1, dyf.at[other])
    gather_end(1)

    n_all = nf[...]
    dy_all = dyf[...].reshape(256, 768)

    def down(hh, j):
        at = [(yy, zp, k) for yy in (0, 2, 1, 3) for zp in range(2) for k in range(3)]
        return jnp.concatenate([piece(g_ref, 2, k, j, yy, 2 * zp + hh)[...] for yy, zp, k in at], axis=0)

    def up_pair(n):
        return jnp.concatenate([weight(1, 2 * n), weight(1, 2 * n + 1)], axis=1)

    def down_pair(n):
        return jnp.concatenate(
            [jnp.concatenate([down(0, 2 * n + m), down(1, 2 * n + m)], axis=1) for m in range(2)], axis=0
        )

    root = 0.7978845608028654

    @pl.loop(0, 2)
    def _(j):
        pre = dot(n_all, up_pair(j))
        squared = pre * pre
        bent = jnp.tanh(root * pre * (1.0 + 0.044715 * squared))
        act[j] = (0.5 * pre * (1.0 + bent)).astype(BF16)
        slope[j] = 0.5 * (1.0 + bent) + 0.5 * pre * (1.0 - bent * bent) * (root * (1.0 + 0.134145 * squared))

    @pl.loop(0, 2)
    def _(j):
        grad = dot(turned(act[j]), dy_all).astype(BF16)
        for m in range(2):
            for hh in range(2):
                for n, yy in enumerate((0, 2, 1, 3)):
                    for zp in range(2):
                        for k in range(3):
                            at = 384 * m + 96 * n + 48 * zp + 16 * k
                            tile = grad[at : at + 16, 384 * hh : 384 * hh + 384]
                            piece(r_ref, 2, k, 2 * j + m, yy, 2 * zp + hh)[...] = tile

    reduce_far(2)
    gather_end(2)

    @pl.loop(0, 2)
    def _(j):
        dpre[j] = (dot_nt(dy_all, down_pair(j)) * slope[j]).astype(BF16)

    def some_rows(j, n):
        at = [divmod(t, 3) for t in range(16 * n, 16 * n + 16)]
        return jnp.concatenate([piece(g_ref, 1, k, *units[u], j)[...] for u, k in at], axis=0)

    def send_grad_normed(n):
        exchange((6, 4, 5)[n], dnp.at[n, other_rows], dnx.at[n])

    for n in range(3):
        part = [
            dot_nt(dpre[j], jnp.concatenate([some_rows(2 * j, n), some_rows(2 * j + 1, n)], axis=1))
            for j in range(2)
        ]
        dnp[n] = part[0] + part[1]
        send_grad_normed(n)

    xhat, inv = normal(hid_ref[own_rows, :])
    for n in range(3):
        exchanged((6, 4, 5)[n], dnx.at[n])
    grad_normed = jnp.concatenate([dnp[n, own_rows, :] + dnx[n] for n in range(3)], axis=1)
    put_rows(
        1,
        jnp.sum(grad_normed * xhat, axis=0, keepdims=True),
        jnp.sum(grad_normed, axis=0, keepdims=True),
    )
    grad_hat = grad_normed * gain
    grad_ln = inv * (
        grad_hat
        - jnp.mean(grad_hat, axis=1, keepdims=True)
        - xhat * jnp.mean(grad_hat * xhat, axis=1, keepdims=True)
    )
    grad_hidden = dyf[c].astype(F32) + grad_ln
    dtok_ref[...] = grad_hidden
    dhf[c] = grad_hidden.astype(BF16)
    exchange(7, dhf.at[c], dhf.at[c])
    own_columns = pl.ds(pl.multiple_of(384 * c, 128), 384)
    other_columns = pl.ds(pl.multiple_of(384 * other, 128), 384)
    dh_sides = jnp.concatenate([dhf[c, :, own_columns], dhf[c, :, other_columns]], axis=1)
    flat = dot(jnp.concatenate([weight(0, 3), other_half(units)], axis=1), turned(dh_sides)).astype(BF16)
    for h in range(12):
        dot_s[h] = flat[64 * h : 64 * h + 64]

    def send_head_grads():
        for n in range(12):
            h = lax.rem(turn + n, 12)
            dev, mine = owner_place(h // 6, 6 * c + lax.rem(h, 6))
            send_or_copy(dot_s.at[h], ado.at[blk], do_s.at[h], do_r.at[blk], dev, mine)

    send_head_grads()
    rows_stage(1, 0)
    turn_ref[...] = turned(n_all)

    @pl.loop(0, 2)
    def _(j):
        grad = dot(turn_ref[...], dpre[j]).astype(BF16)
        put(1, 2 * j, units, grad[:, 0:384])
        put(1, 2 * j + 1, units, grad[:, 384:768])

    exchanged(7, dhf.at[other])
    dh_own = dhf[:, :, own_columns].reshape(256, 384)
    reduce_near(2)
    reduce_far(1)

    @pl.loop(0, 2)
    def _(hh):
        grad = dot(turned(of[hh]), dh_own).astype(BF16)
        put(0, 3, [(2 * hh + n, py) for n in range(2) for py in range(4)], grad)


    @pl.when(owner)
    def _():
        dkt[...] = jnp.zeros_like(dkt)
        dvt[...] = jnp.zeros_like(dvt)

    def backward_step(ii, kt, on_diagonal):
        queries = blocks_of(aq, 4 * ii, 4, 0)
        grads = blocks_of(ado, 4 * ii, 4)
        bias = 0.0 if on_diagonal else split_bias(ii, kt)
        grad_s = [[], []]
        for n in range(2):
            tile = 2 * kt + n
            h0 = n if on_diagonal else 0
            lanes = slice(TILE * h0, 2 * TILE)
            scores = dot(kn[tile], queries[:, lanes])
            grad_w = dot(vn[tile], grads[:, lanes])
            all_weights = []
            for h in range(h0, 2):
                at = slice(TILE * (h - h0), TILE * (h - h0) + TILE)
                signs = sign_of(scores[:, at])
                probs = jnp.exp2(jnp.abs(scores[:, at]) * EXP_SCALE - (lse_ref[2 * ii + h] - bias))
                if on_diagonal and h == n:
                    probs = jnp.where(key_at <= query_at, probs, 0.0)
                weights = probs * signs
                all_weights.append(weights.astype(BF16))
                grad_s[n].append((weights * (signs * grad_w[:, at] - delta_ref[h])).astype(BF16))
            dkt[tile] += dot_nt(queries[:, lanes], jnp.concatenate(grad_s[n], axis=1))
            dvt[tile] += dot_nt(grads[:, lanes], jnp.concatenate(all_weights, axis=1))
        for h in range(2):
            terms = [g[h - len(g)] if on_diagonal else g[h] for g in grad_s if len(g) + h >= 2]
            keys = blocks_of(aq, 4 * kt, 2 * len(terms), 1)
            term = dot(keys, jnp.concatenate(terms, axis=0))
            if on_diagonal:
                acc_ref[h] = term
            else:
                acc_ref[h] += term

    def backward_first(ii):
        for b in range(4):
            landed(ado.at[4 * ii + b], do_r.at[4 * ii + b])
        for h in range(2):
            grads = blocks_of(ado, 4 * ii + 2 * h, 2).astype(F32)
            delta_ref[h] = jnp.sum(grads * otf[2 * ii + h], axis=0, keepdims=True)
        backward_step(ii, ii, True)

    def backward_last(ii):
        for h in range(2):
            grad_q = (acc_ref[h] * SCALE).astype(BF16)
            grad_k = (dkt[2 * ii + h] * SCALE).astype(BF16)
            grad_v = dvt[2 * ii + h].astype(BF16)
            for b in range(2):
                at = 4 * ii + 2 * h + b
                lanes = slice(128 * b, 128 * b + 128)
                dqs[at, 0] = grad_q[:, lanes]
                dqs[at, 1] = grad_k[:, lanes]
                dqs[at, 2] = grad_v[:, lanes]
        for n in range(4):
            grads_home(4 * ii + lax.rem(z + n, 4))

    def emit_output():
        exchanged(8, dxr)
        out_ref[...] = (hid_ref[own_rows, :] + pdown[own_rows, :] + dxr[...]).astype(BF16)
        pltpu.make_async_copy(out_ref, out_hbm, in_s.at[0]).start()

    run_steps(
        backward_first,
        backward_step,
        backward_last,
        {},
        {(0, 2): lambda: reduce_near(1)},
    )

    to_core = lax.rem(y, 2)

    def send_sums(b):
        for s in range(8):
            if not drain:
                fin_s[b, s, 0:6, :] = p_ref[b, 6 * s : 6 * s + 6, :]
                fin_s[b, s, 6:8, :] = jnp.zeros((2, 384), F32)
            to_y = 2 * (y // 2) + s // 4
            mine = (c == to_core) & (y == to_y) & (z == s % 4)
            dev, at = place(x, to_core, to_y, s % 4), c * 4 + z
            send_or_copy(
                fin_s.at[b, s], fin_r.at[b, at], fin_ss.at[9 * b + s], fin_rs.at[9 * b + at], dev, mine
            )
        if b == 1:
            if not drain:
                fds[...] = p_ref[2, pl.ds(pl.multiple_of(24 * (1 - half), 8), 24), :]
            send(fds, fdr, fin_ss.at[8], fin_rs.at[8], partner)

    for m in range(HEADS_HERE):
        landed(dqh.at[m], dq_r.at[m])
    @pl.loop(0, 3)
    def _(j):
        halves_of = [jnp.concatenate([dqh[6 * g + h, j] for h in range(6)], axis=0) for g in range(2)]
        dqf[j] = jnp.concatenate(halves_of, axis=1)
        put(0, j, units, dot_nt(xt_ref[...], dqf[j]).astype(BF16))

    reduce_far(0)
    reduce_end(2)
    reduce_small(2, 1)
    reduce_end(1)
    reduce_small(1, 1)
    rows_sum(1, 0)
    rows_stage(1, 1)

    @pl.loop(0, 3)
    def _(j):
        term = dot(weight(0, j), dqf[j])
        for g in range(2):
            lanes = slice(128 * g, 128 * g + 128)
            dtp[g] = jnp.where(j == 0, term[:, lanes], dtp[g] + term[:, lanes])

    exchange(9, dtp.at[other], dtx)
    reduce_near(0)
    reduce_small_end(2, 1)
    reduce_small(2, 0)
    reduce_small_end(1, 1)
    reduce_small(1, 0)

    pdown[...] = dot(act[0], down_pair(0))
    pdown[...] += dot(act[1], down_pair(1))
    exchange(8, pdown.at[other_rows], dxr)
    rows_sum(1, 1)
    reduce_small_end(2, 0)
    reduce_small_end(1, 0)
    send_sums(1)
    reduce_end(0)
    reduce_plane(0)
    exchanged(9, dtx)
    dtok_ref[...] = dtok_ref[...] + (dtp[c] + dtx[...]).T
    pltpu.make_async_copy(dtok_ref, dtok_hbm, in_s.at[1]).start()
    drain.append(True)
    exchanges()
    send_strips()
    send_heads()
    send_head_grads()
    for b in range(3):
        gather_near(b)
        gather_far(b)
        reduce_far(b)
        reduce_near(b)
        for p in range(2):
            if b > 0:
                gather_small(b, p)
                reduce_small(b, p)
    gather_plane(0)
    for u in range(2):
        for stage in range(2):
            rows_stage(u, stage)

    @pl.when(owner)
    def _():
        @pl.loop(0, 16)
        def _(b):
            heads_home(b)
            grads_home(b)

    drain.clear()
    emit_output()
    reduce_plane_end(0)

    send_sums(0)
    kept = p_ref[2, pl.ds(pl.multiple_of(24 * half, 8), 24), :]
    gather_row = lax.broadcasted_iota(jnp.int32, (768, 128), 0)
    gather_lane = lax.broadcasted_iota(jnp.int32, (768, 128), 1)
    pick = jnp.where((gather_row == first + gather_lane) & (gather_lane < 6), 1.0, 0.0)
    sums_of_rows = jnp.concatenate(get_rows(1) + [jnp.zeros((6, 768), F32)], axis=0)
    dgs_ref[...] = lax.dot_general(
        sums_of_rows, pick, (((1,), (0,)), ((), ())), precision=lax.Precision.HIGHEST, preferred_element_type=F32
    )
    landed(fdr, fin_rs.at[8])
    ddown_ref[:, 0:384] = jnp.where(half == 0, kept, fdr[...])
    ddown_ref[:, 384:768] = jnp.where(half == 0, fdr[...], kept)
    for b in range(2):
        for at in range(8):
            landed(fin_r.at[b, at], fin_rs.at[9 * b + at])

    pltpu.make_async_copy(out_ref, out_hbm, in_s.at[0]).wait()
    pltpu.make_async_copy(dtok_ref, dtok_hbm, in_s.at[1]).wait()
    drain.append(True)
    reduce_plane(0)
    send_sums(0)
    send_sums(1)


def write_results(out_ref, dtok_ref, dgs_ref, fin_ref, ddown_ref, *results):
    output, d_tokens, d_qkv, d_out, d_gain, d_shift, d_up, d_down = results
    output[...] = out_ref[...]
    d_tokens[...] = dtok_ref[...]
    d_gain[...] = dgs_ref[0:1, 0:6]
    d_shift[...] = dgs_ref[1:2, 0:6]
    d_down[...] = ddown_ref[...]
    for at in range(8):
        cc, zz = at // 4, at % 4
        if zz < 3:
            d_qkv[:, 768 * zz + 384 * cc : 768 * zz + 384 * cc + 384] = fin_ref[0, at, 0:6, :]
        else:
            d_out[:, 384 * cc : 384 * cc + 384] = fin_ref[0, at, 0:6, :]
        f0 = 384 * (2 * zz + cc)
        d_up[:, f0 : f0 + 384] = fin_ref[1, at, 0:6, :]


def layer(tokens, lengths, w_qkv, w_out, norm_gain, norm_shift, w_up, w_down, cotangent):
    rows, width = tokens.shape[1], tokens.shape[2]
    vmem = pl.BlockSpec(memory_space=pltpu.VMEM)
    hbm = pl.BlockSpec(memory_space=pl.ANY)
    dma = pltpu.SemaphoreType.DMA
    scratch = [
        (w_qkv.shape, BF16),
        (w_out.shape, BF16),
        (w_up.shape, BF16),
        (w_down.shape, BF16),
        ((rows, width), BF16),
        ((rows, width), F32),
        ((3, 3, 4, 4, 4, 16, 384), BF16),
        ((3, 3, 4, 4, 4, 16, 384), BF16),
        ((3, 3, 2, 2, 4, 16, 384), BF16),
        ((3, 3, 2, 4, 4, 16, 384), BF16),
        ((3, 3, 3, 4, 16, 384), BF16),
        ((3, 3, 3, 16, 384), BF16),
        ((3, 15, 16, 384), BF16),
        ((3, 48, 384), F32),
        ((2, 128, 768), BF16),
        ((2, 128, 768), BF16),
        ((2, 8, TILE), F32),
        ((2, 8, 8, 384), F32),
        ((2, 8, 8, 384), F32),
        ((2, 48, 384), F32),
        ((24, 384), F32),
        ((24, 384), F32),
        ((48, 384), F32),
        ((2, 3, 8, 256), F32),
        ((2, 22, 8, 256), F32),
        ((3, 4, 4, 16, 384), BF16),
        ((HEADS_HERE, 3, 64, 128), BF16),
        ((16, 3, 64, 128), BF16),
        ((TILES, TILE, 64), BF16),
        ((TILES, TILE, 64), BF16),
        ((TILES, 64, TILE), F32),
        ((TILES, 1, TILE), F32),
        ((2, 1, TILE), F32),
        ((2, 1, TILE), F32),
        ((2, 1, TILE), F32),
        ((2, 64, TILE), F32),
        ((16, 64, 128), BF16),
        ((2, HEADS_HERE, 64, 128), BF16),
        ((2, 256, 384), BF16),
        ((256, 768), BF16),
        ((2, 256, 768), BF16),
        ((2, 256, 768), F32),
        ((768, 256), BF16),
        ((768, 256), BF16),
        ((2, 256, 768), BF16),
        ((256, 768), F32),
        ((128, 768), F32),
        ((3, 256, 256), F32),
        ((3, 128, 256), F32),
        ((2, 128, 768), BF16),
        ((HEADS_HERE, 64, 128), BF16),
        ((16, 64, 128), BF16),
        ((TILES, 64, TILE), F32),
        ((TILES, 64, TILE), F32),
        ((16, 3, 64, 128), BF16),
        ((HEADS_HERE, 3, 64, 128), BF16),
        ((3, 384, 256), BF16),
        ((2, 768, 128), F32),
        ((768, 128), F32),
        ((256, 768), F32),
        ((2, 8, 8, 384), F32),
        ((24, 384), F32),
        ((24, 384), F32),
    ]
    sems = [
        (108,), (108,), (54,), (54,), (108,), (108,), (54,), (54,), (3, 15), (3, 15), (3, 15), (3, 15), (17,), (17,), (12,), (12,), (2, 22), (2, 22),
        (12,), (16,), (2, 16), (2, 12), (12,), (16,), (16,), (12,), (17,), (17,), (6,),
    ]
    results = pl.pallas_call(
        kernel,
        out_shape=(
            jax.ShapeDtypeStruct((rows, width), BF16),
            jax.ShapeDtypeStruct((rows, width), F32),
            jax.ShapeDtypeStruct((8, 128), F32),
            jax.ShapeDtypeStruct((2, 8, 8, 384), F32),
            jax.ShapeDtypeStruct(w_down.shape, F32),
        ),
        in_specs=[hbm, pl.BlockSpec(memory_space=pltpu.SMEM), hbm, hbm, vmem, vmem, hbm, hbm, hbm],
        out_specs=[hbm, hbm, vmem, vmem, vmem],
        scratch_shapes=[pltpu.VMEM(s, t) for s, t in scratch] + [dma(s) for s in sems],
        compiler_params=pltpu.CompilerParams(
            collective_id=0, has_side_effects=True, vmem_limit_bytes=56 * 1024 * 1024
        ),
    )(
        tokens.reshape(rows, width), lengths, w_qkv, w_out, norm_gain.reshape(1, 6), norm_shift.reshape(1, 6),
        w_up, w_down, cotangent.reshape(rows, width),
    )
    output, d_tokens, d_qkv, d_out, d_gain, d_shift, d_up, d_down = pl.pallas_call(
        write_results,
        out_shape=(
            jax.ShapeDtypeStruct((rows, width), BF16),
            jax.ShapeDtypeStruct((rows, width), F32),
            jax.ShapeDtypeStruct(w_qkv.shape, F32),
            jax.ShapeDtypeStruct(w_out.shape, F32),
            jax.ShapeDtypeStruct((1, 6), F32),
            jax.ShapeDtypeStruct((1, 6), F32),
            jax.ShapeDtypeStruct(w_up.shape, F32),
            jax.ShapeDtypeStruct(w_down.shape, F32),
        ),
        in_specs=[vmem] * 5,
        out_specs=[vmem] * 8,
    )(*results)
    return (
        output.reshape(1, rows, width),
        d_tokens.reshape(1, rows, width),
        d_qkv,
        d_out,
        d_gain.reshape(6),
        d_shift.reshape(6),
        d_up,
        d_down,
    )


def solution(mesh):
    by_token = P("dp", "blk", None)
    by_row = P(("dp", "blk"), None)
    by_entry = P(("dp", "blk"))
    return jax.shard_map(
        layer,
        mesh=mesh,
        in_specs=(by_token, P("dp"), by_row, by_row, by_entry, by_entry, by_row, by_row, by_token),
        out_specs=(by_token, by_token, by_row, by_row, by_entry, by_entry, by_row, by_row),
        check_vma=False,
    )
```
